32 devices in a mesh: lon: 4 (over x, core), lat: 2 (over y), head: 4 (over z).
Axes of the slice: x: 2, y: 2, z: 4, core: 2. Of those that a mesh axis runs over, the one named last changes fastest.
Arguments:
- tokens: bfloat16 [48, 48, 4, 512], P('lon', 'lat', None, 'head'), may hold values from -6 to 6
- qkv_weight: bfloat16 [2, 3, 512, 512], P(None, None, None, 'head')
- out_weight: bfloat16 [2, 512, 512], P(None, 'head'), may hold values from -0.25 to 0.25
- up_weight: bfloat16 [2, 512, 2048], P(None, None, 'head'), may hold values from -0.25 to 0.25
- down_weight: bfloat16 [2, 2048, 512], P(None, 'head'), may hold values from -0.125 to 0.125
- bias_table: float32 [2, 759, 8], P(None, None, 'head'), may hold values from -4 to 4
- bias_index: int32 [144, 144], replicated, may hold values from 0 to 758
- regions: int32 [48, 48, 4], P('lon', 'lat'), may hold values from 0 to 7, as said below
Outputs:
- state: bfloat16 [48, 48, 4, 512], P('lon', 'lat', None, 'head')
The draws below stay inside these ranges and needn't reach their ends.
Inputs may be any that keep to these rules, and one draw needn't show every extreme that they name: regions is a class id (0 to 3): 2 if the latitude row is among the first 3, plus 1 if the level is 0.
All inputs are finite; a program needn't handle non-finite values.
Results may differ from the reference program's by a relative error of at most 0.02.
Values may be sent and summed in bfloat16 or wider, within the bound.
A program may use at most 64 MiB of HBM per device.

```python
import math
import jax
import jax.numpy as jnp
from jax import lax

D = 512
HEADS = 8
FF = 2048
WIN_LON = 12
WIN_LAT = 6
WIN_LEV = 2
LEV = 4
WIN_TOK = 144
BIAS_ROWS = 759
NLON = 48
NLAT = 48
N_HEAD = 4


def draw_qkv_weight(key, part):
    key = jax.random.fold_in(key, 11)
    weight = jax.random.normal(key, (2, 3, D, D), jnp.float32) / math.sqrt(D)
    return weight.astype(jnp.bfloat16)


def draw_regions(key, part):
    key = jax.random.fold_in(key, 5)
    shape = (NLON, NLAT, LEV)
    column_bits = jax.random.randint(key, (NLON, NLAT, 1), 0, 2, jnp.int32)
    lat_pos = lax.broadcasted_iota(jnp.int32, shape, 1)
    lev_pos = lax.broadcasted_iota(jnp.int32, shape, 2)
    top = (lat_pos < WIN_LAT // 2).astype(jnp.int32)
    bottom = (lev_pos == 0).astype(jnp.int32)
    return (4 * column_bits + 2 * top + bottom).astype(jnp.int32)


def plant(result, own_key, least, top_value):
    place = [jax.random.randint(jax.random.fold_in(own_key, axis), (), 0, length) for axis, length in enumerate(result.shape)]
    longest = result.shape.index(max(result.shape))
    beside = place[:longest] + [(place[longest] + 1) % result.shape[longest]] + place[longest + 1:]
    return result.at[tuple(place)].set(least).at[tuple(beside)].set(top_value)


def shard_levels(own_key, shape, shards, low, largest):
    gain = 1.0
    for axis_at, shards_of in shards:
        steps = jax.random.uniform(jax.random.fold_in(jax.random.fold_in(own_key, 6), axis_at), (shards_of,), jnp.float32, low / len(shards), largest / len(shards))
        gain = gain * jnp.repeat(jnp.exp(steps), shape[axis_at] // shards_of).reshape((-1,) + (1,) * (len(shape) - 1 - axis_at))
    return gain


def normal_values(rng, extent, scale, limit, cuts=(), dtype=jnp.bfloat16):
    entries = scale * jax.random.normal(rng, extent, jnp.float32)
    if cuts:
        entries = entries * shard_levels(rng, extent, cuts, -0.22, 0.18)
    return jnp.clip(entries, -limit, limit).astype(dtype)


def setup_inputs(seed: int = 0) -> dict:
    splits = jax.random.split(jax.random.key(seed), 9)
    tokens = normal_values(splits[0], (NLON, NLAT, LEV, D), 1.0, 6.0, ((0, 4), (1, 2), (3, 4)))
    qkv_weight = draw_qkv_weight(jax.random.fold_in(splits[8], 71), 0)
    out_weight = normal_values(splits[2], (2, D, D), D ** -0.5, 0.25, ((1, 4),))
    up_weight = normal_values(splits[3], (2, D, FF), D ** -0.5, 0.25, ((2, 4),))
    down_weight = normal_values(splits[4], (2, FF, D), FF ** -0.5, 0.125, ((1, 4),))
    bias_table = normal_values(splits[5], (2, BIAS_ROWS, HEADS), 1.0, 4.0, ((2, 4),), jnp.float32)
    bias_index = plant(jax.random.randint(splits[6], (WIN_TOK, WIN_TOK), 0, BIAS_ROWS), jax.random.fold_in(splits[6], 1), 0, BIAS_ROWS - 1).astype(jnp.int32)
    regions = draw_regions(jax.random.fold_in(splits[8], 71), 0)
    return dict(tokens=tokens, qkv_weight=qkv_weight, out_weight=out_weight, up_weight=up_weight, down_weight=down_weight, bias_table=bias_table, bias_index=bias_index, regions=regions)


EPS = 1e-05
MASKED = -1000000000.0

def layer_norm(values):
    values = values.astype(jnp.float32)
    center = values - lax.optimization_barrier(jnp.mean(values, axis=-1, keepdims=True))
    spread = lax.optimization_barrier(jnp.mean(center * center, axis=-1, keepdims=True))
    return (center * lax.rsqrt(spread + EPS)).astype(jnp.bfloat16)

def split_windows(arr):
    lon_n, lat_n, lev_n, cols = arr.shape
    arr = arr.reshape(lon_n // WIN_LON, WIN_LON, lat_n // WIN_LAT, WIN_LAT, lev_n // WIN_LEV, WIN_LEV, cols)
    arr = arr.transpose(0, 2, 4, 1, 3, 5, 6)
    return arr.reshape(-1, WIN_LON * WIN_LAT * WIN_LEV, cols)

def join_windows(arr, lon_n, lat_n, lev_n):
    cols = arr.shape[-1]
    arr = arr.reshape(lon_n // WIN_LON, lat_n // WIN_LAT, lev_n // WIN_LEV, WIN_LON, WIN_LAT, WIN_LEV, cols)
    arr = arr.transpose(0, 3, 1, 4, 2, 5, 6)
    return arr.reshape(lon_n, lat_n, lev_n, cols)

def attend(normed, weight, table, index, marks):
    lon_n, lat_n, lev_n, width = normed.shape
    heads = table.shape[1]
    cols = weight.shape[2]
    head_dim = cols // heads
    merged = jnp.einsum('lavd,tdc->tlavc', normed.astype(jnp.float32), weight.astype(jnp.float32)).astype(jnp.bfloat16)
    query = split_windows(merged[0])
    count = query.shape[0]
    query = query.reshape(count, -1, heads, head_dim)
    keys = split_windows(merged[1]).reshape(count, -1, heads, head_dim)
    values = split_windows(merged[2]).reshape(count, -1, heads, head_dim)
    bias = jnp.take(table, index, axis=0).transpose(2, 0, 1)
    scores = jnp.einsum('wqhe,wkhe->whqk', query.astype(jnp.float32), keys.astype(jnp.float32))
    scores = scores * head_dim ** (-0.5) + bias[None]
    if marks is not None:
        flat = split_windows(marks[..., None])[..., 0]
        same = flat[:, :, None] == flat[:, None, :]
        scores = jnp.where(same[:, None], scores, MASKED)
    scores = scores - lax.optimization_barrier(jnp.max(scores, axis=-1, keepdims=True))
    expo = jnp.exp(scores)
    probs = (expo / lax.optimization_barrier(jnp.sum(expo, axis=-1, keepdims=True))).astype(jnp.bfloat16)
    out = jnp.einsum('whqk,wkhe->wqhe', probs.astype(jnp.float32), values.astype(jnp.float32)).astype(jnp.bfloat16)
    return join_windows(out.reshape(count, -1, cols), lon_n, lat_n, lev_n)

def group_sum(mixed, weight):
    cols = mixed.shape[-1]
    split = mixed.reshape(mixed.shape[:-1] + (N_HEAD, cols // N_HEAD))
    rows = weight.reshape(N_HEAD, cols // N_HEAD, weight.shape[1])
    parts = jnp.einsum('lavgc,gcd->lavgd', split.astype(jnp.float32), rows.astype(jnp.float32))
    parts = lax.optimization_barrier(parts.astype(jnp.bfloat16))
    return lax.optimization_barrier(jnp.sum(parts.astype(jnp.float32), axis=3))

def reference(tokens, qkv_weight, out_weight, up_weight, down_weight, bias_table, bias_index, regions):
    state = tokens
    slab_shape = (NLON // WIN_LON, WIN_LON, NLAT, LEV)
    offsets = (-(WIN_LON // 2), -(WIN_LAT // 2), -1)
    for block in range(2):
        shifted = block == 1
        normed = layer_norm(state)
        marks = regions
        if shifted:
            normed = jnp.roll(normed, offsets, axis=(0, 1, 2))
            marks = jnp.roll(marks, offsets, axis=(0, 1, 2))

        def attn_slab(pair):
            slab, slab_marks = pair
            mixed = attend(slab, qkv_weight[block], bias_table[block], bias_index, slab_marks if shifted else None)
            return group_sum(mixed, out_weight[block])
        total = lax.map(attn_slab, (normed.reshape(slab_shape + (D,)), marks.reshape(slab_shape)))
        total = total.reshape(NLON, NLAT, LEV, D)
        if shifted:
            total = jnp.roll(total, tuple((-o for o in offsets)), axis=(0, 1, 2))
        state = (state.astype(jnp.float32) + total).astype(jnp.bfloat16)
        normed = layer_norm(state)

        def mlp_slab(slab):
            hidden = jax.nn.gelu(jnp.dot(slab, up_weight[block], preferred_element_type=jnp.float32)).astype(jnp.bfloat16)
            return group_sum(hidden, down_weight[block])
        total = lax.map(mlp_slab, normed.reshape(slab_shape + (D,))).reshape(NLON, NLAT, LEV, D)
        state = (state.astype(jnp.float32) + total).astype(jnp.bfloat16)
    return state
```

```python
import functools

import jax
import jax.numpy as jnp
import numpy as np
from jax import lax
from jax.experimental import pallas as pl
from jax.experimental.pallas import tpu as pltpu
from jax.sharding import PartitionSpec as P

WIN_LON = 12
WIN_LAT = 6
WIN_LEV = 2
LEV = 4
TOK = WIN_LON * WIN_LAT * WIN_LEV
ROWS = 2 * TOK
QUAD = 80
EPS = 1e-05
MASKED = -1000000000.0
HEADS_N = 4
MESH = pl.DeviceIdType.MESH


def row_maps():
    to_quads = np.zeros((4 * QUAD, ROWS), np.float32)
    to_rolled = np.zeros((ROWS, 4 * QUAD), np.float32)
    for w in range(2):
        for lon in range(12):
            for lat in range(6):
                for lv in range(2):
                    row = ((w * 12 + lon) * 6 + lat) * 2 + lv
                    lev = 2 * w + lv
                    quad = (lon // 6) * 2 + lat // 3
                    at = quad * QUAD + ((lon % 6) * 3 + lat % 3) * 4 + lev
                    to_quads[at, row] = 1
                    src_lon, src_lat, src_lev = (lon + 6) % 12, (lat + 3) % 6, (lev + 1) % 4
                    quad = (src_lon // 6) * 2 + src_lat // 3
                    at = quad * QUAD + ((src_lon % 6) * 3 + src_lat % 3) * 4 + src_lev
                    to_rolled[row, at] = 1
    return to_quads, to_rolled


def norm(values):
    center = values - jnp.mean(values, axis=-1, keepdims=True)
    spread = jnp.mean(center * center, axis=-1, keepdims=True)
    return (center * lax.rsqrt(spread + EPS)).astype(jnp.bfloat16)


def dot(a, b):
    return jnp.dot(a, b, preferred_element_type=jnp.float32)


def kernel(
    nlon, nlat,
    x_ref, qw_ref, ow_ref, uw_ref, dw_ref, tab_ref, idx_ref, oh_ref, quads_ref, rolled_ref, back_ref,
    out_ref,
    xp, wq, wo, wu, wd, tabs, bias, nb, ho, acc, st, same, hsend, hrecv, ysend,
    own_sem, xs_sem, xr_sem, ts_sem, tr_sem, zs_sem, zr_sem, ps_sem, pr_sem, cs_sem, cr_sem,
    hs_sem, hr_sem, ys_sem, or_sem,
):
    lon, lat, head = lax.axis_index("lon"), lax.axis_index("lat"), lax.axis_index("head")

    def at(d_lon, d_lat, to_head):
        return (lax.rem(lon + d_lon + nlon, nlon), lax.rem(lat + d_lat + nlat, nlat), to_head)

    core = lax.rem(lon, 2)
    xbit = lax.rem(lon // 2, 2)
    ybit = lax.rem(lat, 2)
    x_lon = lon + 2 - 4 * xbit
    y_lat = lat + 1 - 2 * ybit
    c_lon = lon + 1 - 2 * core

    barrier = pltpu.get_barrier_semaphore()
    count = 0
    for d_lon in (-1, 0, 1):
        for d_lat in (-1, 0, 1):
            for k in range(HEADS_N):
                if d_lon == 0 and d_lat == 0 and k == 0:
                    continue
                pl.semaphore_signal(
                    barrier, inc=1, device_id=at(d_lon, d_lat, lax.rem(head + k, HEADS_N)), device_id_type=MESH
                )
                count += 1
    for target in ((x_lon, lat, head), (x_lon, y_lat, head), (lon, y_lat, head)):
        pl.semaphore_signal(barrier, inc=1, device_id=target, device_id_type=MESH)
        count += 1
    pl.semaphore_wait(barrier, count)

    def remote(src, dst, send, recv, target):
        return pltpu.make_async_remote_copy(
            src_ref=src, dst_ref=dst, send_sem=send, recv_sem=recv, device_id=target, device_id_type=MESH
        )

    weights = ((qw_ref, wq), (ow_ref, wo), (uw_ref, wu), (dw_ref, wd))

    def part(ref, which):
        rows = ref.shape[2] // 8
        return pl.ds(pl.multiple_of(which * rows, 16), rows)

    mine = core * 4 + xbit * 2 + ybit
    of_x = core * 4 + (1 - xbit) * 2 + ybit
    of_y = core * 4 + xbit * 2 + 1 - ybit
    of_d = core * 4 + (1 - xbit) * 2 + 1 - ybit

    def x_copy(k):
        to = lax.rem(head + k, HEADS_N)
        return remote(x_ref.at[to], xp.at[head], xs_sem.at[k], xr_sem.at[k], (lon, lat, to))

    def t_copy(k):
        to = lax.rem(head + k, HEADS_N)
        return remote(tab_ref, tabs.at[head], ts_sem.at[k], tr_sem.at[k], (lon, lat, to))

    def z_copy(b, i, k):
        src, dst = weights[i]
        rows = part(dst, mine)
        to = lax.rem(head + k, HEADS_N)
        return remote(
            src.at[b, rows], dst.at[b, head, rows], zs_sem.at[b, i, k - 1], zr_sem.at[b, i, k - 1], (lon, lat, to)
        )

    def source(k):
        return lax.rem(head + HEADS_N - k, HEADS_N)

    def z_landed(b, i, k):
        dst = weights[i][1].at[b, source(k), part(weights[i][1], mine)]
        pltpu.make_async_copy(dst, dst, zr_sem.at[b, i, k - 1]).wait()

    def p_copies(b, i, k):
        ref = weights[i][1].at[b, source(k), part(weights[i][1], mine)]
        targets = ((x_lon, lat, head), (lon, y_lat, head), (x_lon, y_lat, head))
        return [
            remote(ref, ref, ps_sem.at[b, i, k - 1, d], pr_sem.at[b, i, k - 1, d], target)
            for d, target in enumerate(targets)
        ]

    def p_landed(b, i, k):
        for d, which in enumerate((of_x, of_y, of_d)):
            dst = weights[i][1].at[b, source(k), part(weights[i][1], which)]
            pltpu.make_async_copy(dst, dst, pr_sem.at[b, i, k - 1, d]).wait()

    def half(ref, which):
        rows = ref.shape[2] // 2
        return pl.ds(pl.multiple_of(which * rows, 16), rows)

    def c_copy(b, i, k):
        ref = weights[i][1].at[b, source(k), half(weights[i][1], core)]
        return remote(ref, ref, cs_sem.at[b, i, k - 1], cr_sem.at[b, i, k - 1], (c_lon, lat, head))

    def c_landed(b, i, k):
        dst = weights[i][1].at[b, source(k), half(weights[i][1], 1 - core)]
        pltpu.make_async_copy(dst, dst, cr_sem.at[b, i, k - 1]).wait()

    def each_k(body):
        def step(k, carry):
            body(k)
            return carry

        lax.fori_loop(1, HEADS_N, step, 0)

    def own_copies():
        copies = [
            pltpu.make_async_copy(src, dst.at[:, head], own_sem.at[i]) for i, (src, dst) in enumerate(weights)
        ]
        copies.append(pltpu.make_async_copy(x_ref.at[head], xp.at[head], own_sem.at[4]))
        copies.append(pltpu.make_async_copy(tab_ref, tabs.at[head], own_sem.at[5]))
        return copies

    each_k(lambda k: t_copy(k).start())
    each_k(lambda k: x_copy(k).start())
    for b in range(2):
        for i in range(4):
            each_k(lambda k: z_copy(b, i, k).start())
    for copy in own_copies():
        copy.start()
    for copy in own_copies():
        copy.wait()

    def forward_plane(b, i):
        def body(k):
            z_landed(b, i, k)
            for copy in p_copies(b, i, k):
                copy.start()

        each_k(body)

    def forward_core(b, i):
        def body(k):
            p_landed(b, i, k)
            c_copy(b, i, k).start()

        each_k(body)

    def arrived(b, i):
        each_k(lambda k: c_landed(b, i, k))

    def make_bias():
        index = idx_ref[...]
        low = jnp.bitwise_and(index, 127)
        high = jnp.right_shift(index, 7)

        def column(j, carry):
            s, c = j // 4, lax.rem(j, 4)
            for side in range(2):
                lanes = slice(side * 128, side * 128 + 128)
                lo, hi = low[:, lanes], high[:, lanes]
                got = jnp.zeros((TOK, 128), jnp.float32)
                for r in range(6):
                    row = jnp.broadcast_to(tabs[s, c, r : r + 1, :], (TOK, 128))
                    got = jnp.where(hi == r, jnp.take_along_axis(row, lo, axis=1, mode="promise_in_bounds"), got)
                bias[j, :, lanes] = got
            return carry

        lax.fori_loop(0, 16, column, 0)

    def attention(b):
        acc[...] = jnp.zeros_like(acc)

        def shard(s, carry):
            n = nb[...]
            q = dot(n, wq[b, s, 0:512, :]).astype(jnp.bfloat16)
            k = dot(n, wq[b, s, 512:1024, :]).astype(jnp.bfloat16)
            v = dot(n, wq[b, s, 1024:1536, :]).astype(jnp.bfloat16)
            for w in range(2):
                rows = slice(w * TOK, (w + 1) * TOK)
                outs = []
                for hh in range(2):
                    cols = slice(hh * 64, hh * 64 + 64)
                    scores = lax.dot_general(
                        q[rows, cols], k[rows, cols], (((1,), (1,)), ((), ())), preferred_element_type=jnp.float32
                    )
                    scores = scores * 0.125 + bias[s * 4 + b * 2 + hh, :, 0:TOK]
                    if b == 1:
                        scores = jnp.where(same[w] > 0.5, scores, MASKED)
                    expo = jnp.exp(scores - jnp.max(scores, axis=-1, keepdims=True))
                    probs = (expo / jnp.sum(expo, axis=-1, keepdims=True)).astype(jnp.bfloat16)
                    outs.append(dot(probs, v[rows, cols]).astype(jnp.bfloat16))
                ho[rows, :] = jnp.concatenate(outs, axis=1)
            acc[...] += dot(ho[...], wo[b, s])
            return carry

        lax.fori_loop(0, 4, shard, 0)

    def feed_forward(b):
        acc[...] = jnp.zeros_like(acc)

        def shard(s, carry):
            hidden = jax.nn.gelu(dot(nb[...], wu[b, s]), approximate=True).astype(jnp.bfloat16)
            acc[...] += dot(hidden, wd[b, s])
            return carry

        lax.fori_loop(0, 4, shard, 0)

    def add_total():
        st[...] = (st[...].astype(jnp.float32) + acc[...]).astype(jnp.bfloat16)

    def renorm():
        nb[...] = norm(st[...].astype(jnp.float32))

    for b in range(2):
        for i in range(4):
            forward_plane(b, i)
    each_k(lambda k: pltpu.make_async_copy(tabs.at[source(k)], tabs.at[source(k)], tr_sem.at[k]).wait())
    each_k(lambda k: pltpu.make_async_copy(xp.at[source(k)], xp.at[source(k)], xr_sem.at[k]).wait())
    make_bias()
    for b in range(2):
        for i in range(4):
            forward_core(b, i)
    for b in range(2):
        for i in range(4):
            arrived(b, i)

    st[...] = jnp.concatenate([xp[g] for g in range(4)], axis=1)
    renorm()
    attention(0)
    add_total()
    renorm()
    feed_forward(0)
    add_total()

    hsend[:, 0:512] = dot(quads_ref[...], st[...]).astype(jnp.bfloat16)
    hsend[:, 512:640] = oh_ref[...]
    before = lax.rem(head + HEADS_N - 1, HEADS_N)
    lat_back = jnp.where(head == 0, -1, 0)
    lat_next = jnp.where(head == HEADS_N - 1, 1, 0)
    quad_to = (at(-1, lat_back, before), at(-1, 0, head), at(0, lat_back, before))

    def quad_rows(q):
        return pl.ds(q * QUAD, QUAD)

    halo = [
        remote(hsend.at[quad_rows(q)], hrecv.at[quad_rows(q)], hs_sem.at[q], hr_sem.at[q], quad_to[q])
        for q in range(3)
    ]
    for copy in halo:
        copy.start()
    hrecv[3 * QUAD : 4 * QUAD, :] = hsend[3 * QUAD : 4 * QUAD, :]
    for copy in halo:
        copy.wait()

    rolled = dot(rolled_ref[...], hrecv[...]).astype(jnp.bfloat16)
    st[...] = rolled[:, 0:512]
    marks = rolled[:, 512:640]
    for w in range(2):
        of_window = marks[w * TOK : (w + 1) * TOK]
        same[w] = lax.dot_general(
            of_window, of_window, (((1,), (1,)), ((), ())), preferred_element_type=jnp.float32
        )
    renorm()
    attention(1)
    add_total()
    renorm()
    feed_forward(1)
    add_total()

    final = dot(back_ref[...], st[...]).astype(jnp.bfloat16)
    for f in range(4):
        ysend[f] = final[:, f * 128 : (f + 1) * 128]
    after = lax.rem(head + 1, HEADS_N)
    homes = ((1, lat_next, after), (1, 0, head), (0, lat_next, after), (0, 0, head))

    def y_copy(q, k):
        d_lon, d_lat, slot = homes[q]
        to = lax.rem(head + k, HEADS_N)
        return remote(
            ysend.at[to, quad_rows(q)], out_ref.at[slot, quad_rows(q)], ys_sem.at[q, k], or_sem.at[slot, q],
            at(d_lon, d_lat, to),
        )

    def y_local(q):
        slot = homes[q][2]
        return pltpu.make_async_copy(
            ysend.at[head, quad_rows(q)], out_ref.at[slot, quad_rows(q)], or_sem.at[slot, q]
        )

    for q in range(4):
        each_k(lambda k: y_copy(q, k).start())
    for q in (0, 1):
        y_copy(q, 0).start()
    y_local(3).start()

    @pl.when(head < HEADS_N - 1)
    def _():
        y_local(2).start()

    @pl.when(head == HEADS_N - 1)
    def _():
        y_copy(2, 0).start()

    each_k(lambda k: t_copy(k).wait_send())
    each_k(lambda k: x_copy(k).wait_send())
    for b in range(2):
        for i in range(4):

            def sent(k):
                z_copy(b, i, k).wait_send()
                for copy in p_copies(b, i, k):
                    copy.wait_send()
                c_copy(b, i, k).wait_send()

            each_k(sent)
    for q in range(4):
        each_k(lambda k: y_copy(q, k).wait_send())
    for q in (0, 1):
        y_copy(q, 0).wait_send()

    @pl.when(head == HEADS_N - 1)
    def _():
        y_copy(2, 0).wait_send()

    for g in range(4):
        for q in range(4):
            dst = out_ref.at[g, quad_rows(q)]
            pltpu.make_async_copy(dst, dst, or_sem.at[g, q]).wait()


def local(
    nlon, nlat, tokens, qkv_weight, out_weight, up_weight, down_weight, bias_table, bias_index, regions
):
    bf16 = jnp.bfloat16
    head = lax.axis_index("head")
    to_quads, to_rolled = row_maps()
    x = tokens.reshape(12, 4, 6, 2, 2, 128).transpose(1, 3, 0, 2, 4, 5).reshape(4, ROWS, 128)
    table = jnp.pad(bias_table, ((0, 0), (0, 1024 - bias_table.shape[1]), (0, 0)))
    table = table.transpose(0, 2, 1).reshape(4, 8, 128)
    index = jnp.pad(bias_index, ((0, 0), (0, 256 - TOK)))
    ids = lax.dynamic_slice_in_dim(regions, head * 6, 6, axis=1)
    ids = ids.reshape(2, 6, 2, 3, 4).transpose(0, 2, 1, 3, 4).reshape(4, 72)
    ids = jnp.pad(ids, ((0, 0), (0, QUAD - 72))).reshape(4 * QUAD, 1)
    marks = (ids == jnp.arange(128, dtype=jnp.int32)[None, :]).astype(bf16)
    sems = pltpu.SemaphoreType.DMA
    vm = pltpu.VMEM
    any_space = pl.BlockSpec(memory_space=pl.ANY)
    in_vmem = pl.BlockSpec(memory_space=pltpu.VMEM)
    out = pl.pallas_call(
        functools.partial(kernel, nlon, nlat),
        out_shape=jax.ShapeDtypeStruct((4, 4 * QUAD, 128), bf16),
        in_specs=[any_space] * 6 + [in_vmem] * 5,
        out_specs=any_space,
        scratch_shapes=[
            vm((4, ROWS, 128), bf16),
            vm((2, 4, 1536, 128), bf16),
            vm((2, 4, 128, 512), bf16),
            vm((2, 4, 512, 512), bf16),
            vm((2, 4, 512, 512), bf16),
            vm((4, 4, 8, 128), jnp.float32),
            vm((16, TOK, 256), jnp.float32),
            vm((ROWS, 512), bf16),
            vm((ROWS, 128), bf16),
            vm((ROWS, 512), jnp.float32),
            vm((ROWS, 512), bf16),
            vm((2, TOK, TOK), jnp.float32),
            vm((4 * QUAD, 640), bf16),
            vm((4 * QUAD, 640), bf16),
            vm((4, 4 * QUAD, 128), bf16),
            sems((6,)),
            sems((4,)),
            sems((4,)),
            sems((4,)),
            sems((4,)),
            sems((2, 4, 3)),
            sems((2, 4, 3)),
            sems((2, 4, 3, 3)),
            sems((2, 4, 3, 3)),
            sems((2, 4, 3)),
            sems((2, 4, 3)),
            sems((3,)),
            sems((3,)),
            sems((4, 4)),
            sems((4, 4)),
        ],
        compiler_params=pltpu.CompilerParams(
            collective_id=0, has_side_effects=True, vmem_limit_bytes=48 * 1024 * 1024
        ),
        name="swin_pair",
    )(
        x,
        qkv_weight.reshape(2, 1536, 128),
        out_weight,
        up_weight,
        down_weight,
        table,
        index,
        marks,
        jnp.asarray(to_quads, bf16),
        jnp.asarray(to_rolled, bf16),
        jnp.asarray(to_rolled.T, bf16),
    )
    out = out.reshape(4, 4, QUAD, 128)[:, :, :72].reshape(4, 2, 2, 6, 3, 4, 128)
    return out.transpose(1, 3, 0, 2, 4, 5, 6).reshape(12, 24, 4, 128)


def solution(mesh):
    return jax.shard_map(
        functools.partial(local, mesh.shape["lon"], mesh.shape["lat"]),
        mesh=mesh,
        in_specs=(
            P("lon", "lat", None, "head"),
            P(None, None, None, "head"),
            P(None, "head", None),
            P(None, None, "head"),
            P(None, "head", None),
            P(None, None, "head"),
            P(),
            P("lon", "lat", None),
        ),
        out_specs=P("lon", "lat", None, "head"),
        check_vma=False,
    )
```

```python
import functools

import jax
import jax.numpy as jnp
import numpy as np
from jax import lax
from jax.experimental import pallas as pl
from jax.experimental.pallas import tpu as pltpu
from jax.sharding import PartitionSpec as P

WIN_LON = 12
WIN_LAT = 6
WIN_LEV = 2
LEV = 4
TOK = WIN_LON * WIN_LAT * WIN_LEV
ROWS = 2 * TOK
QUAD = 80
EPS = 1e-05
MASKED = -1000000000.0
HEADS_N = 4
MESH = pl.DeviceIdType.MESH


def row_maps():
    to_quads = np.zeros((4 * QUAD, ROWS), np.float32)
    to_rolled = np.zeros((ROWS, 4 * QUAD), np.float32)
    for w in range(2):
        for lon in range(12):
            for lat in range(6):
                for lv in range(2):
                    row = ((w * 12 + lon) * 6 + lat) * 2 + lv
                    lev = 2 * w + lv
                    quad = (lon // 6) * 2 + lat // 3
                    at = quad * QUAD + ((lon % 6) * 3 + lat % 3) * 4 + lev
                    to_quads[at, row] = 1
                    src_lon, src_lat, src_lev = (lon + 6) % 12, (lat + 3) % 6, (lev + 1) % 4
                    quad = (src_lon // 6) * 2 + src_lat // 3
                    at = quad * QUAD + ((src_lon % 6) * 3 + src_lat % 3) * 4 + src_lev
                    to_rolled[row, at] = 1
    return to_quads, to_rolled


def norm(values):
    center = values - jnp.mean(values, axis=-1, keepdims=True)
    spread = jnp.mean(center * center, axis=-1, keepdims=True)
    return (center * lax.rsqrt(spread + EPS)).astype(jnp.bfloat16)


def dot(a, b):
    return jnp.dot(a, b, preferred_element_type=jnp.float32)


def kernel(
    nlon, nlat,
    x_ref, qw_ref, ow_ref, uw_ref, dw_ref, tab_ref, idx_hbm, oh_hbm, quads_hbm, rolled_hbm, back_hbm,
    out_ref,
    idx_ref, quads_ref, rolled_ref, back_ref, xp, wq, wo, wu, wd, tabs, bias, nb, ho, acc, st, same, hsend, hrecv, ysend,
    own_sem, xs_sem, xr_sem, ts_sem, tr_sem, zs_sem, zr_sem, ps_sem, pr_sem, cs_sem, cr_sem,
    hs_sem, hr_sem, ys_sem, or_sem,
):
    lon, lat, head = lax.axis_index("lon"), lax.axis_index("lat"), lax.axis_index("head")

    def at(d_lon, d_lat, to_head):
        return (lax.rem(lon + d_lon + nlon, nlon), lax.rem(lat + d_lat + nlat, nlat), to_head)

    core = lax.rem(lon, 2)
    xbit = lax.rem(lon // 2, 2)
    ybit = lax.rem(lat, 2)
    x_lon = lon + 2 - 4 * xbit
    y_lat = lat + 1 - 2 * ybit
    c_lon = lon + 1 - 2 * core

    barrier = pltpu.get_barrier_semaphore()
    count = 0
    for d_lon in (-1, 0, 1):
        for d_lat in (-1, 0, 1):
            for k in range(HEADS_N):
                if d_lon == 0 and d_lat == 0 and k == 0:
                    continue
                pl.semaphore_signal(
                    barrier, inc=1, device_id=at(d_lon, d_lat, lax.rem(head + k, HEADS_N)), device_id_type=MESH
                )
                count += 1
    for target in ((x_lon, lat, head), (x_lon, y_lat, head), (lon, y_lat, head)):
        pl.semaphore_signal(barrier, inc=1, device_id=target, device_id_type=MESH)
        count += 1

    def remote(src, dst, send, recv, target):
        return pltpu.make_async_remote_copy(
            src_ref=src, dst_ref=dst, send_sem=send, recv_sem=recv, device_id=target, device_id_type=MESH
        )

    weights = ((qw_ref, wq), (ow_ref, wo), (uw_ref, wu), (dw_ref, wd))

    def part(ref, which):
        rows = ref.shape[2] // 8
        return pl.ds(pl.multiple_of(which * rows, 16), rows)

    mine = core * 4 + xbit * 2 + ybit
    of_x = core * 4 + (1 - xbit) * 2 + ybit
    of_y = core * 4 + xbit * 2 + 1 - ybit
    of_d = core * 4 + (1 - xbit) * 2 + 1 - ybit

    def x_copy(k):
        to = lax.rem(head + k, HEADS_N)
        return remote(x_ref.at[to], xp.at[head], xs_sem.at[k], xr_sem.at[k], (lon, lat, to))

    def t_copy(k):
        to = lax.rem(head + k, HEADS_N)
        return remote(tab_ref, tabs.at[head], ts_sem.at[k], tr_sem.at[k], (lon, lat, to))

    def z_copy(b, i, k):
        src, dst = weights[i]
        rows = part(dst, mine)
        to = lax.rem(head + k, HEADS_N)
        return remote(
            src.at[b, rows], dst.at[b, head, rows], zs_sem.at[b, i, k - 1], zr_sem.at[b, i, k - 1], (lon, lat, to)
        )

    def source(k):
        return lax.rem(head + HEADS_N - k, HEADS_N)

    def z_landed(b, i, k):
        dst = weights[i][1].at[b, source(k), part(weights[i][1], mine)]
        pltpu.make_async_copy(dst, dst, zr_sem.at[b, i, k - 1]).wait()

    def p_copies(b, i, k):
        ref = weights[i][1].at[b, source(k), part(weights[i][1], mine)]
        return [
            remote(ref, ref, ps_sem.at[b, i, k - 1, d], pr_sem.at[b, i, k - 1, d], target)
            for d, target in enumerate(((x_lon, lat, head), (lon, y_lat, head)))
        ]

    def p_landed(b, i, k, d):
        dst = weights[i][1].at[b, source(k), part(weights[i][1], (of_x, of_y, of_d)[d])]
        pltpu.make_async_copy(dst, dst, pr_sem.at[b, i, k - 1, d]).wait()

    def d_copy(b, i, k):
        by_x = lax.rem(b + i + k, 2)
        ref = weights[i][1].at[b, source(k), part(weights[i][1], by_x * of_x + (1 - by_x) * of_y)]
        target = (by_x * lon + (1 - by_x) * x_lon, by_x * y_lat + (1 - by_x) * lat, head)
        return remote(ref, ref, ps_sem.at[b, i, k - 1, 2], pr_sem.at[b, i, k - 1, 2], target)

    def half(ref, which):
        rows = ref.shape[2] // 2
        return pl.ds(pl.multiple_of(which * rows, 16), rows)

    def c_copy(b, i, k):
        ref = weights[i][1].at[b, source(k), half(weights[i][1], core)]
        return remote(ref, ref, cs_sem.at[b, i, k - 1], cr_sem.at[b, i, k - 1], (c_lon, lat, head))

    def c_landed(b, i, k):
        dst = weights[i][1].at[b, source(k), half(weights[i][1], 1 - core)]
        pltpu.make_async_copy(dst, dst, cr_sem.at[b, i, k - 1]).wait()

    def each_k(body):
        def step(k, carry):
            body(k)
            return carry

        lax.fori_loop(1, HEADS_N, step, 0)

    def own_copies():
        copies = [
            pltpu.make_async_copy(src, dst.at[:, head], own_sem.at[i]) for i, (src, dst) in enumerate(weights)
        ]
        copies.append(pltpu.make_async_copy(x_ref.at[head], xp.at[head], own_sem.at[4]))
        copies.append(pltpu.make_async_copy(tab_ref, tabs.at[head], own_sem.at[5]))
        small = (
            (idx_hbm, idx_ref), (quads_hbm, quads_ref), (rolled_hbm, rolled_ref), (back_hbm, back_ref),
            (oh_hbm, hsend.at[:, 512:640]),
        )
        for i, (src, dst) in enumerate(small):
            copies.append(pltpu.make_async_copy(src, dst, own_sem.at[6 + i]))
        return copies

    for copy in own_copies():
        copy.start()
    pl.semaphore_wait(barrier, count)
    each_k(lambda k: t_copy(k).start())
    each_k(lambda k: x_copy(k).start())
    for b in range(2):
        for i in range(4):
            each_k(lambda k: z_copy(b, i, k).start())
    for copy in own_copies():
        copy.wait()

    def forward_plane(b, i):
        def body(k):
            z_landed(b, i, k)
            for copy in p_copies(b, i, k):
                copy.start()

        each_k(body)

    def forward_diagonal(b, i):
        def body(k):
            p_landed(b, i, k, 0)
            p_landed(b, i, k, 1)
            d_copy(b, i, k).start()

        each_k(body)

    def forward_core(b, i):
        def body(k):
            p_landed(b, i, k, 2)
            c_copy(b, i, k).start()

        each_k(body)

    def plan():
        order = [(b, i) for b in range(2) for i in range(4)]
        for step in range(len(order) + 2):
            for late, forward in enumerate((forward_plane, forward_diagonal, forward_core)):
                if 0 <= step - late < len(order):
                    yield forward, order[step - late]

    pending = list(plan())

    def pump(count):
        for forward, (b, i) in pending[:count]:
            forward(b, i)
        del pending[:count]

    def make_bias(k):
        s = source(k)
        index = idx_ref[...]
        edge = jnp.concatenate([index[:, 128:], jnp.zeros((TOK, 256 - TOK), jnp.int32)], axis=1)

        def column(c, carry):
            for side, part_index in enumerate((index[:, :128], edge)):
                lo = jnp.bitwise_and(part_index, 127)
                hi = jnp.right_shift(part_index, 7)
                got = jnp.zeros((TOK, 128), jnp.float32)
                for r in range(6):
                    row = jnp.broadcast_to(tabs[s, c, r : r + 1, :], (TOK, 128))
                    got = jnp.where(hi == r, jnp.take_along_axis(row, lo, axis=1, mode="promise_in_bounds"), got)
                bias[s * 4 + c, :, side * 128 : side * 128 + 128] = got
            return carry

        lax.fori_loop(0, 4, column, 0)

    def attention(b, k):
        s = source(k)
        n = nb[...]
        query = dot(n, wq[b, s, 0:512, :]).astype(jnp.bfloat16)
        keys = dot(n, wq[b, s, 512:1024, :]).astype(jnp.bfloat16)
        v = dot(n, wq[b, s, 1024:1536, :]).astype(jnp.bfloat16)
        for w in range(2):
            rows = slice(w * TOK, (w + 1) * TOK)
            outs = []
            for hh in range(2):
                cols = slice(hh * 64, hh * 64 + 64)
                scores = lax.dot_general(
                    query[rows, cols], keys[rows, cols], (((1,), (1,)), ((), ())),
                    preferred_element_type=jnp.float32,
                )
                scores = scores * 0.125 + bias[s * 4 + b * 2 + hh, :, 0:TOK]
                if b == 1:
                    scores = jnp.where(same[w] > 0.5, scores, MASKED)
                expo = jnp.exp(scores - jnp.max(scores, axis=-1, keepdims=True))
                probs = (expo / jnp.sum(expo, axis=-1, keepdims=True)).astype(jnp.bfloat16)
                outs.append(dot(probs, v[rows, cols]).astype(jnp.bfloat16))
            ho[rows, :] = jnp.concatenate(outs, axis=1)
        total = dot(ho[...], wo[b, s])
        acc[...] = total if k == 0 else acc[...] + total

    def feed_forward(b, k):
        s = source(k)
        hidden = jax.nn.gelu(dot(nb[...], wu[b, s]), approximate=True).astype(jnp.bfloat16)
        total = dot(hidden, wd[b, s])
        acc[...] = total if k == 0 else acc[...] + total

    def add_total():
        st[...] = (st[...].astype(jnp.float32) + acc[...]).astype(jnp.bfloat16)

    def renorm():
        nb[...] = norm(st[...].astype(jnp.float32))

    pump(1)
    each_k(lambda k: pltpu.make_async_copy(xp.at[source(k)], xp.at[source(k)], xr_sem.at[k]).wait())
    st[...] = jnp.concatenate([xp[g] for g in range(4)], axis=1)
    renorm()
    pump(2)
    make_bias(0)
    pump(3)
    attention(0, 0)
    pump(3)
    each_k(lambda k: pltpu.make_async_copy(tabs.at[source(k)], tabs.at[source(k)], tr_sem.at[k]).wait())
    make_bias(1)
    pump(3)
    make_bias(2)
    make_bias(3)
    for k in range(1, 4):
        c_landed(0, 0, k)
        c_landed(0, 1, k)
        attention(0, k)
        pump(2)
    add_total()
    renorm()
    for k in range(4):
        if k > 0:
            c_landed(0, 2, k)
            c_landed(0, 3, k)
        feed_forward(0, k)
        pump(2)
    add_total()

    hsend[:, 0:512] = dot(quads_ref[...], st[...]).astype(jnp.bfloat16)
    before = lax.rem(head + HEADS_N - 1, HEADS_N)
    lat_back = jnp.where(head == 0, -1, 0)
    lat_next = jnp.where(head == HEADS_N - 1, 1, 0)
    quad_to = (at(-1, lat_back, before), at(-1, 0, head), at(0, lat_back, before))

    def quad_rows(q):
        return pl.ds(q * QUAD, QUAD)

    halo = [
        remote(hsend.at[quad_rows(q)], hrecv.at[quad_rows(q)], hs_sem.at[q], hr_sem.at[q], quad_to[q])
        for q in range(3)
    ]
    for copy in halo:
        copy.start()
    hrecv[3 * QUAD : 4 * QUAD, :] = hsend[3 * QUAD : 4 * QUAD, :]
    for copy in halo:
        copy.wait()

    rolled = dot(rolled_ref[...], hrecv[...]).astype(jnp.bfloat16)
    st[...] = rolled[:, 0:512]
    marks = rolled[:, 512:640]
    for w in range(2):
        of_window = marks[w * TOK : (w + 1) * TOK]
        same[w] = lax.dot_general(
            of_window, of_window, (((1,), (1,)), ((), ())), preferred_element_type=jnp.float32
        )
    renorm()
    attention(1, 0)
    pump(len(pending))
    for k in range(1, 4):
        c_landed(1, 0, k)
        c_landed(1, 1, k)
        attention(1, k)
    add_total()
    renorm()
    for k in range(4):
        if k > 0:
            c_landed(1, 2, k)
            c_landed(1, 3, k)
        feed_forward(1, k)
    add_total()

    final = dot(back_ref[...], st[...]).astype(jnp.bfloat16)
    for f in range(4):
        ysend[f] = final[:, f * 128 : (f + 1) * 128]
    after = lax.rem(head + 1, HEADS_N)
    homes = ((1, lat_next, after), (1, 0, head), (0, lat_next, after), (0, 0, head))

    def y_copy(q, k):
        d_lon, d_lat, slot = homes[q]
        to = lax.rem(head + k, HEADS_N)
        return remote(
            ysend.at[to, quad_rows(q)], out_ref.at[slot, quad_rows(q)], ys_sem.at[q, k], or_sem.at[slot, q],
            at(d_lon, d_lat, to),
        )

    def y_local(q):
        slot = homes[q][2]
        return pltpu.make_async_copy(
            ysend.at[head, quad_rows(q)], out_ref.at[slot, quad_rows(q)], or_sem.at[slot, q]
        )

    for q in range(4):
        each_k(lambda k: y_copy(q, k).start())
    for q in (0, 1):
        y_copy(q, 0).start()
    y_local(3).start()

    @pl.when(head < HEADS_N - 1)
    def _():
        y_local(2).start()

    @pl.when(head == HEADS_N - 1)
    def _():
        y_copy(2, 0).start()

    each_k(lambda k: t_copy(k).wait_send())
    each_k(lambda k: x_copy(k).wait_send())
    for b in range(2):
        for i in range(4):

            def sent(k):
                z_copy(b, i, k).wait_send()
                for copy in p_copies(b, i, k):
                    copy.wait_send()
                d_copy(b, i, k).wait_send()
                c_copy(b, i, k).wait_send()

            each_k(sent)
    for q in range(4):
        each_k(lambda k: y_copy(q, k).wait_send())
    for q in (0, 1):
        y_copy(q, 0).wait_send()

    @pl.when(head == HEADS_N - 1)
    def _():
        y_copy(2, 0).wait_send()

    for g in range(4):
        for q in range(4):
            dst = out_ref.at[g, quad_rows(q)]
            pltpu.make_async_copy(dst, dst, or_sem.at[g, q]).wait()


def local(
    nlon, nlat, tokens, qkv_weight, out_weight, up_weight, down_weight, bias_table, bias_index, regions
):
    bf16 = jnp.bfloat16
    head = lax.axis_index("head")
    to_quads, to_rolled = row_maps()
    x = tokens.reshape(12, 4, 6, 2, 2, 128).transpose(1, 3, 0, 2, 4, 5).reshape(4, ROWS, 128)
    table = jnp.pad(bias_table, ((0, 0), (0, 1024 - bias_table.shape[1]), (0, 0)))
    table = table.transpose(0, 2, 1).reshape(4, 8, 128)
    ids = lax.dynamic_slice_in_dim(regions, head * 6, 6, axis=1)
    ids = ids.reshape(2, 6, 2, 3, 4).transpose(0, 2, 1, 3, 4).reshape(4, 72)
    ids = jnp.pad(ids, ((0, 0), (0, QUAD - 72))).reshape(4 * QUAD, 1)
    marks = (ids == jnp.arange(128, dtype=jnp.int32)[None, :]).astype(bf16)
    sems = pltpu.SemaphoreType.DMA
    vm = pltpu.VMEM
    any_space = pl.BlockSpec(memory_space=pl.ANY)
    in_hbm = pl.BlockSpec(memory_space=pltpu.HBM)
    out = pl.pallas_call(
        functools.partial(kernel, nlon, nlat),
        out_shape=jax.ShapeDtypeStruct((4, 4 * QUAD, 128), bf16),
        in_specs=[any_space] + [in_hbm] * 4 + [any_space] + [in_hbm] + [any_space] + [in_hbm] * 3,
        out_specs=any_space,
        scratch_shapes=[
            vm((TOK, TOK), jnp.int32),
            vm((4 * QUAD, ROWS), bf16),
            vm((ROWS, 4 * QUAD), bf16),
            vm((4 * QUAD, ROWS), bf16),
            vm((4, ROWS, 128), bf16),
            vm((2, 4, 1536, 128), bf16),
            vm((2, 4, 128, 512), bf16),
            vm((2, 4, 512, 512), bf16),
            vm((2, 4, 512, 512), bf16),
            vm((4, 4, 8, 128), jnp.float32),
            vm((16, TOK, 256), jnp.float32),
            vm((ROWS, 512), bf16),
            vm((ROWS, 128), bf16),
            vm((ROWS, 512), jnp.float32),
            vm((ROWS, 512), bf16),
            vm((2, TOK, TOK), jnp.float32),
            vm((4 * QUAD, 640), bf16),
            vm((4 * QUAD, 640), bf16),
            vm((4, 4 * QUAD, 128), bf16),
            sems((11,)),
            sems((4,)),
            sems((4,)),
            sems((4,)),
            sems((4,)),
            sems((2, 4, 3)),
            sems((2, 4, 3)),
            sems((2, 4, 3, 3)),
            sems((2, 4, 3, 3)),
            sems((2, 4, 3)),
            sems((2, 4, 3)),
            sems((3,)),
            sems((3,)),
            sems((4, 4)),
            sems((4, 4)),
        ],
        compiler_params=pltpu.CompilerParams(
            collective_id=0, has_side_effects=True, vmem_limit_bytes=48 * 1024 * 1024
        ),
        name="swin_pair",
    )(
        x,
        qkv_weight.reshape(2, 1536, 128),
        out_weight,
        up_weight,
        down_weight,
        table,
        bias_index,
        marks,
        jnp.asarray(to_quads, bf16),
        jnp.asarray(to_rolled, bf16),
        jnp.asarray(to_rolled.T, bf16),
    )
    out = out.reshape(4, 4, QUAD, 128)[:, :, :72].reshape(4, 2, 2, 6, 3, 4, 128)
    return out.transpose(1, 3, 0, 2, 4, 5, 6).reshape(12, 24, 4, 128)


def solution(mesh):
    return jax.shard_map(
        functools.partial(local, mesh.shape["lon"], mesh.shape["lat"]),
        mesh=mesh,
        in_specs=(
            P("lon", "lat", None, "head"),
            P(None, None, None, "head"),
            P(None, "head", None),
            P(None, None, "head"),
            P(None, "head", None),
            P(None, None, "head"),
            P(),
            P("lon", "lat", None),
        ),
        out_specs=P("lon", "lat", None, "head"),
        check_vma=False,
    )
```

```python
import functools

import jax
import jax.numpy as jnp
import numpy as np
from jax import lax
from jax.experimental import pallas as pl
from jax.experimental.pallas import tpu as pltpu
from jax.sharding import PartitionSpec as P

WIN_LON = 12
WIN_LAT = 6
WIN_LEV = 2
LEV = 4
TOK = WIN_LON * WIN_LAT * WIN_LEV
ROWS = 2 * TOK
QUAD = 80
EPS = 1e-05
MASKED = -1000000000.0
HEADS_N = 4
MESH = pl.DeviceIdType.MESH


def row_maps():
    to_quads = np.zeros((4 * QUAD, ROWS), np.float32)
    to_rolled = np.zeros((ROWS, 4 * QUAD), np.float32)
    for w in range(2):
        for lon in range(12):
            for lat in range(6):
                for lv in range(2):
                    row = ((w * 12 + lon) * 6 + lat) * 2 + lv
                    lev = 2 * w + lv
                    quad = (lon // 6) * 2 + lat // 3
                    at = quad * QUAD + ((lon % 6) * 3 + lat % 3) * 4 + lev
                    to_quads[at, row] = 1
                    src_lon, src_lat, src_lev = (lon + 6) % 12, (lat + 3) % 6, (lev + 1) % 4
                    quad = (src_lon // 6) * 2 + src_lat // 3
                    at = quad * QUAD + ((src_lon % 6) * 3 + src_lat % 3) * 4 + src_lev
                    to_rolled[row, at] = 1
    return to_quads, to_rolled


def norm(values):
    center = values - jnp.mean(values, axis=-1, keepdims=True)
    spread = jnp.mean(center * center, axis=-1, keepdims=True)
    return (center * lax.rsqrt(spread + EPS)).astype(jnp.bfloat16)


def dot(a, b):
    return jnp.dot(a, b, preferred_element_type=jnp.float32)


def kernel(
    nlon, nlat,
    x_ref, qw_ref, ow_ref, uw_ref, dw_ref, tab_ref, idx_hbm, oh_hbm, quads_hbm, rolled_hbm, back_hbm,
    out_ref,
    idx_ref, quads_ref, rolled_ref, back_ref, xp, wq, wo, wu, wd, tabs, bias, nb, ho, acc, st, same, hsend, hrecv, ysend,
    own_sem, xs_sem, xr_sem, ts_sem, tr_sem, zs_sem, zr_sem, ps_sem, pr_sem, cs_sem, cr_sem,
    hs_sem, hr_sem, ys_sem, or_sem,
):
    lon, lat, head = lax.axis_index("lon"), lax.axis_index("lat"), lax.axis_index("head")

    def at(d_lon, d_lat, to_head):
        return (lax.rem(lon + d_lon + nlon, nlon), lax.rem(lat + d_lat + nlat, nlat), to_head)

    core = lax.rem(lon, 2)
    xbit = lax.rem(lon // 2, 2)
    ybit = lax.rem(lat, 2)
    x_lon = lon + 2 - 4 * xbit
    y_lat = lat + 1 - 2 * ybit
    c_lon = lon + 1 - 2 * core

    barrier = pltpu.get_barrier_semaphore()
    count = 0
    for d_lon in (-1, 0, 1):
        for d_lat in (-1, 0, 1):
            for k in range(HEADS_N):
                if d_lon == 0 and d_lat == 0 and k == 0:
                    continue
                pl.semaphore_signal(
                    barrier, inc=1, device_id=at(d_lon, d_lat, lax.rem(head + k, HEADS_N)), device_id_type=MESH
                )
                count += 1
    for target in ((x_lon, lat, head), (x_lon, y_lat, head), (lon, y_lat, head)):
        pl.semaphore_signal(barrier, inc=1, device_id=target, device_id_type=MESH)
        count += 1

    def remote(src, dst, send, recv, target):
        return pltpu.make_async_remote_copy(
            src_ref=src, dst_ref=dst, send_sem=send, recv_sem=recv, device_id=target, device_id_type=MESH
        )

    weights = ((qw_ref, wq), (ow_ref, wo), (uw_ref, wu), (dw_ref, wd))

    def part(ref, which):
        rows = ref.shape[2] // 8
        return pl.ds(pl.multiple_of(which * rows, 16), rows)

    mine = core * 4 + xbit * 2 + ybit
    of_x = core * 4 + (1 - xbit) * 2 + ybit
    of_y = core * 4 + xbit * 2 + 1 - ybit
    of_d = core * 4 + (1 - xbit) * 2 + 1 - ybit

    def x_copy(k):
        to = lax.rem(head + k, HEADS_N)
        return remote(x_ref.at[to], xp.at[head], xs_sem.at[k], xr_sem.at[k], (lon, lat, to))

    def t_copy(k):
        to = lax.rem(head + k, HEADS_N)
        return remote(tab_ref, tabs.at[head], ts_sem.at[k], tr_sem.at[k], (lon, lat, to))

    def z_copy(b, i, k):
        src, dst = weights[i]
        rows = part(dst, mine)
        to = lax.rem(head + k, HEADS_N)
        return remote(
            src.at[b, rows], dst.at[b, head, rows], zs_sem.at[b, i, k - 1], zr_sem.at[b, i, k - 1], (lon, lat, to)
        )

    def source(k):
        return lax.rem(head + HEADS_N - k, HEADS_N)

    def z_landed(b, i, k):
        dst = weights[i][1].at[b, source(k), part(weights[i][1], mine)]
        pltpu.make_async_copy(dst, dst, zr_sem.at[b, i, k - 1]).wait()

    def p_copies(b, i, k):
        ref = weights[i][1].at[b, source(k), part(weights[i][1], mine)]
        return [
            remote(ref, ref, ps_sem.at[b, i, k - 1, d], pr_sem.at[b, i, k - 1, d], target)
            for d, target in enumerate(((x_lon, lat, head), (lon, y_lat, head)))
        ]

    def p_landed(b, i, k, d):
        dst = weights[i][1].at[b, source(k), part(weights[i][1], (of_x, of_y, of_d)[d])]
        pltpu.make_async_copy(dst, dst, pr_sem.at[b, i, k - 1, d]).wait()

    def d_copy(b, i, k):
        by_x = lax.rem(b + i + k, 2)
        ref = weights[i][1].at[b, source(k), part(weights[i][1], by_x * of_x + (1 - by_x) * of_y)]
        target = (by_x * lon + (1 - by_x) * x_lon, by_x * y_lat + (1 - by_x) * lat, head)
        return remote(ref, ref, ps_sem.at[b, i, k - 1, 2], pr_sem.at[b, i, k - 1, 2], target)

    def half(ref, which):
        rows = ref.shape[2] // 2
        return pl.ds(pl.multiple_of(which * rows, 16), rows)

    def c_copy(b, i, k):
        ref = weights[i][1].at[b, source(k), half(weights[i][1], core)]
        return remote(ref, ref, cs_sem.at[b, i, k - 1], cr_sem.at[b, i, k - 1], (c_lon, lat, head))

    def c_landed(b, i, k):
        dst = weights[i][1].at[b, source(k), half(weights[i][1], 1 - core)]
        pltpu.make_async_copy(dst, dst, cr_sem.at[b, i, k - 1]).wait()

    def each_k(body):
        def step(k, carry):
            body(k)
            return carry

        lax.fori_loop(1, HEADS_N, step, 0)

    def own_copies():
        copies = [
            pltpu.make_async_copy(src, dst.at[:, head], own_sem.at[i]) for i, (src, dst) in enumerate(weights)
        ]
        copies.append(pltpu.make_async_copy(x_ref.at[head], xp.at[head], own_sem.at[4]))
        copies.append(pltpu.make_async_copy(tab_ref, tabs.at[head], own_sem.at[5]))
        small = (
            (idx_hbm, idx_ref), (quads_hbm, quads_ref), (rolled_hbm, rolled_ref), (back_hbm, back_ref),
            (oh_hbm, hsend.at[:, 512:640]),
        )
        for i, (src, dst) in enumerate(small):
            copies.append(pltpu.make_async_copy(src, dst, own_sem.at[6 + i]))
        return copies

    for copy in own_copies():
        copy.start()
    pl.semaphore_wait(barrier, count)
    each_k(lambda k: t_copy(k).start())
    each_k(lambda k: x_copy(k).start())
    order = [(b, i) for b in range(2) for i in range(4)]
    ahead = 2

    def send_along_z(t):
        if t < len(order):
            each_k(lambda k: z_copy(*order[t], k).start())

    for t in range(ahead):
        send_along_z(t)
    for copy in own_copies():
        copy.wait()

    def forward_plane(b, i):
        def body(k):
            z_landed(b, i, k)
            for copy in p_copies(b, i, k):
                copy.start()

        each_k(body)
        send_along_z(order.index((b, i)) + ahead)

    def forward_diagonal(b, i):
        def body(k):
            p_landed(b, i, k, 0)
            p_landed(b, i, k, 1)
            d_copy(b, i, k).start()

        each_k(body)

    def forward_core(b, i):
        def body(k):
            p_landed(b, i, k, 2)
            c_copy(b, i, k).start()

        each_k(body)

    def plan():
        for step in range(len(order) + 2):
            for late, forward in enumerate((forward_plane, forward_diagonal, forward_core)):
                if 0 <= step - late < len(order):
                    yield forward, order[step - late]

    pending = list(plan())

    def pump(count):
        for forward, (b, i) in pending[:count]:
            forward(b, i)
        del pending[:count]

    def make_bias(k):
        s = source(k)
        index = idx_ref[...]
        edge = jnp.concatenate([index[:, 128:], jnp.zeros((TOK, 256 - TOK), jnp.int32)], axis=1)

        def column(c, carry):
            for side, part_index in enumerate((index[:, :128], edge)):
                lo = jnp.bitwise_and(part_index, 127)
                hi = jnp.right_shift(part_index, 7)
                got = jnp.zeros((TOK, 128), jnp.float32)
                for r in range(6):
                    row = jnp.broadcast_to(tabs[s, c, r : r + 1, :], (TOK, 128))
                    got = jnp.where(hi == r, jnp.take_along_axis(row, lo, axis=1, mode="promise_in_bounds"), got)
                bias[s * 4 + c, :, side * 128 : side * 128 + 128] = got
            return carry

        lax.fori_loop(0, 4, column, 0)

    def attention(b, k):
        s = source(k)
        n = nb[...]
        query = dot(n, wq[b, s, 0:512, :]).astype(jnp.bfloat16)
        keys = dot(n, wq[b, s, 512:1024, :]).astype(jnp.bfloat16)
        v = dot(n, wq[b, s, 1024:1536, :]).astype(jnp.bfloat16)
        for w in range(2):
            rows = slice(w * TOK, (w + 1) * TOK)
            outs = []
            for hh in range(2):
                cols = slice(hh * 64, hh * 64 + 64)
                scores = lax.dot_general(
                    query[rows, cols], keys[rows, cols], (((1,), (1,)), ((), ())),
                    preferred_element_type=jnp.float32,
                )
                scores = scores * 0.125 + bias[s * 4 + b * 2 + hh, :, 0:TOK]
                if b == 1:
                    scores = jnp.where(same[w] > 0.5, scores, MASKED)
                expo = jnp.exp(scores - jnp.max(scores, axis=-1, keepdims=True))
                probs = (expo / jnp.sum(expo, axis=-1, keepdims=True)).astype(jnp.bfloat16)
                outs.append(dot(probs, v[rows, cols]).astype(jnp.bfloat16))
            ho[rows, :] = jnp.concatenate(outs, axis=1)
        total = dot(ho[...], wo[b, s])
        acc[...] = total if k == 0 else acc[...] + total

    def feed_forward(b, k):
        s = source(k)
        hidden = jax.nn.gelu(dot(nb[...], wu[b, s]), approximate=True).astype(jnp.bfloat16)
        total = dot(hidden, wd[b, s])
        acc[...] = total if k == 0 else acc[...] + total

    def add_total():
        st[...] = (st[...].astype(jnp.float32) + acc[...]).astype(jnp.bfloat16)

    def renorm():
        nb[...] = norm(st[...].astype(jnp.float32))

    pump(1)
    each_k(lambda k: pltpu.make_async_copy(xp.at[source(k)], xp.at[source(k)], xr_sem.at[k]).wait())
    st[...] = jnp.concatenate([xp[g] for g in range(4)], axis=1)
    renorm()
    pump(2)
    make_bias(0)
    pump(3)
    attention(0, 0)
    pump(3)
    each_k(lambda k: pltpu.make_async_copy(tabs.at[source(k)], tabs.at[source(k)], tr_sem.at[k]).wait())
    make_bias(1)
    pump(3)
    make_bias(2)
    make_bias(3)
    for k in range(1, 4):
        c_landed(0, 0, k)
        c_landed(0, 1, k)
        attention(0, k)
        pump(1)
    add_total()
    renorm()
    for k in range(4):
        if k > 0:
            c_landed(0, 2, k)
            c_landed(0, 3, k)
        feed_forward(0, k)
        pump(1)
    add_total()

    hsend[:, 0:512] = dot(quads_ref[...], st[...]).astype(jnp.bfloat16)
    before = lax.rem(head + HEADS_N - 1, HEADS_N)
    lat_back = jnp.where(head == 0, -1, 0)
    lat_next = jnp.where(head == HEADS_N - 1, 1, 0)
    quad_to = (at(-1, lat_back, before), at(-1, 0, head), at(0, lat_back, before))

    def quad_rows(q):
        return pl.ds(q * QUAD, QUAD)

    halo = [
        remote(hsend.at[quad_rows(q)], hrecv.at[quad_rows(q)], hs_sem.at[q], hr_sem.at[q], quad_to[q])
        for q in range(3)
    ]
    for copy in halo:
        copy.start()
    hrecv[3 * QUAD : 4 * QUAD, :] = hsend[3 * QUAD : 4 * QUAD, :]
    pump(2)
    for copy in halo:
        copy.wait()

    rolled = dot(rolled_ref[...], hrecv[...]).astype(jnp.bfloat16)
    st[...] = rolled[:, 0:512]
    marks = rolled[:, 512:640]
    for w in range(2):
        of_window = marks[w * TOK : (w + 1) * TOK]
        same[w] = lax.dot_general(
            of_window, of_window, (((1,), (1,)), ((), ())), preferred_element_type=jnp.float32
        )
    renorm()
    attention(1, 0)
    pump(1)
    for k in range(1, 4):
        c_landed(1, 0, k)
        c_landed(1, 1, k)
        attention(1, k)
        pump(1)
    add_total()
    renorm()
    for k in range(4):
        if k > 0:
            c_landed(1, 2, k)
            c_landed(1, 3, k)
        feed_forward(1, k)
    add_total()

    final = dot(back_ref[...], st[...]).astype(jnp.bfloat16)
    for f in range(4):
        ysend[f] = final[:, f * 128 : (f + 1) * 128]
    after = lax.rem(head + 1, HEADS_N)
    homes = ((1, lat_next, after), (1, 0, head), (0, lat_next, after), (0, 0, head))

    def y_copy(q, k):
        d_lon, d_lat, slot = homes[q]
        to = lax.rem(head + k, HEADS_N)
        return remote(
            ysend.at[to, quad_rows(q)], out_ref.at[slot, quad_rows(q)], ys_sem.at[q, k], or_sem.at[slot, q],
            at(d_lon, d_lat, to),
        )

    def y_local(q):
        slot = homes[q][2]
        return pltpu.make_async_copy(
            ysend.at[head, quad_rows(q)], out_ref.at[slot, quad_rows(q)], or_sem.at[slot, q]
        )

    for q in range(4):
        each_k(lambda k: y_copy(q, k).start())
    for q in (0, 1):
        y_copy(q, 0).start()
    y_local(3).start()

    @pl.when(head < HEADS_N - 1)
    def _():
        y_local(2).start()

    @pl.when(head == HEADS_N - 1)
    def _():
        y_copy(2, 0).start()

    each_k(lambda k: t_copy(k).wait_send())
    each_k(lambda k: x_copy(k).wait_send())
    for b in range(2):
        for i in range(4):

            def sent(k):
                z_copy(b, i, k).wait_send()
                for copy in p_copies(b, i, k):
                    copy.wait_send()
                d_copy(b, i, k).wait_send()
                c_copy(b, i, k).wait_send()

            each_k(sent)
    for q in range(4):
        each_k(lambda k: y_copy(q, k).wait_send())
    for q in (0, 1):
        y_copy(q, 0).wait_send()

    @pl.when(head == HEADS_N - 1)
    def _():
        y_copy(2, 0).wait_send()

    for g in range(4):
        for q in range(4):
            dst = out_ref.at[g, quad_rows(q)]
            pltpu.make_async_copy(dst, dst, or_sem.at[g, q]).wait()


def local(
    nlon, nlat, tokens, qkv_weight, out_weight, up_weight, down_weight, bias_table, bias_index, regions
):
    bf16 = jnp.bfloat16
    head = lax.axis_index("head")
    to_quads, to_rolled = row_maps()
    x = tokens.reshape(12, 4, 6, 2, 2, 128).transpose(1, 3, 0, 2, 4, 5).reshape(4, ROWS, 128)
    table = jnp.pad(bias_table, ((0, 0), (0, 1024 - bias_table.shape[1]), (0, 0)))
    table = table.transpose(0, 2, 1).reshape(4, 8, 128)
    ids = lax.dynamic_slice_in_dim(regions, head * 6, 6, axis=1)
    ids = ids.reshape(2, 6, 2, 3, 4).transpose(0, 2, 1, 3, 4).reshape(4, 72)
    ids = jnp.pad(ids, ((0, 0), (0, QUAD - 72))).reshape(4 * QUAD, 1)
    marks = (ids == jnp.arange(128, dtype=jnp.int32)[None, :]).astype(bf16)
    sems = pltpu.SemaphoreType.DMA
    vm = pltpu.VMEM
    any_space = pl.BlockSpec(memory_space=pl.ANY)
    in_hbm = pl.BlockSpec(memory_space=pltpu.HBM)
    out = pl.pallas_call(
        functools.partial(kernel, nlon, nlat),
        out_shape=jax.ShapeDtypeStruct((4, 4 * QUAD, 128), bf16),
        in_specs=[any_space] + [in_hbm] * 4 + [any_space] + [in_hbm] + [any_space] + [in_hbm] * 3,
        out_specs=any_space,
        scratch_shapes=[
            vm((TOK, TOK), jnp.int32),
            vm((4 * QUAD, ROWS), bf16),
            vm((ROWS, 4 * QUAD), bf16),
            vm((4 * QUAD, ROWS), bf16),
            vm((4, ROWS, 128), bf16),
            vm((2, 4, 1536, 128), bf16),
            vm((2, 4, 128, 512), bf16),
            vm((2, 4, 512, 512), bf16),
            vm((2, 4, 512, 512), bf16),
            vm((4, 4, 8, 128), jnp.float32),
            vm((16, TOK, 256), jnp.float32),
            vm((ROWS, 512), bf16),
            vm((ROWS, 128), bf16),
            vm((ROWS, 512), jnp.float32),
            vm((ROWS, 512), bf16),
            vm((2, TOK, TOK), jnp.float32),
            vm((4 * QUAD, 640), bf16),
            vm((4 * QUAD, 640), bf16),
            vm((4, 4 * QUAD, 128), bf16),
            sems((11,)),
            sems((4,)),
            sems((4,)),
            sems((4,)),
            sems((4,)),
            sems((2, 4, 3)),
            sems((2, 4, 3)),
            sems((2, 4, 3, 3)),
            sems((2, 4, 3, 3)),
            sems((2, 4, 3)),
            sems((2, 4, 3)),
            sems((3,)),
            sems((3,)),
            sems((4, 4)),
            sems((4, 4)),
        ],
        compiler_params=pltpu.CompilerParams(
            collective_id=0, has_side_effects=True, vmem_limit_bytes=48 * 1024 * 1024
        ),
        name="swin_pair",
    )(
        x,
        qkv_weight.reshape(2, 1536, 128),
        out_weight,
        up_weight,
        down_weight,
        table,
        bias_index,
        marks,
        jnp.asarray(to_quads, bf16),
        jnp.asarray(to_rolled, bf16),
        jnp.asarray(to_rolled.T, bf16),
    )
    out = out.reshape(4, 4, QUAD, 128)[:, :, :72].reshape(4, 2, 2, 6, 3, 4, 128)
    return out.transpose(1, 3, 0, 2, 4, 5, 6).reshape(12, 24, 4, 128)


def solution(mesh):
    return jax.shard_map(
        functools.partial(local, mesh.shape["lon"], mesh.shape["lat"]),
        mesh=mesh,
        in_specs=(
            P("lon", "lat", None, "head"),
            P(None, None, None, "head"),
            P(None, "head", None),
            P(None, None, "head"),
            P(None, "head", None),
            P(None, None, "head"),
            P(),
            P("lon", "lat", None),
        ),
        out_specs=P("lon", "lat", None, "head"),
        check_vma=False,
    )
```

```python
import functools

import jax
import jax.numpy as jnp
import numpy as np
from jax import lax
from jax.experimental import pallas as pl
from jax.experimental.pallas import tpu as pltpu
from jax.sharding import PartitionSpec as P

WIN_LON = 12
WIN_LAT = 6
WIN_LEV = 2
LEV = 4
TOK = WIN_LON * WIN_LAT * WIN_LEV
ROWS = 2 * TOK
QUAD = 80
EPS = 1e-05
MASKED = -1000000000.0
HEADS_N = 4
MESH = pl.DeviceIdType.MESH


def row_maps():
    to_quads = np.zeros((4 * QUAD, ROWS), np.float32)
    to_rolled = np.zeros((ROWS, 4 * QUAD), np.float32)
    for w in range(2):
        for lon in range(12):
            for lat in range(6):
                for lv in range(2):
                    row = ((w * 12 + lon) * 6 + lat) * 2 + lv
                    lev = 2 * w + lv
                    quad = (lon // 6) * 2 + lat // 3
                    at = quad * QUAD + ((lon % 6) * 3 + lat % 3) * 4 + lev
                    to_quads[at, row] = 1
                    src_lon, src_lat, src_lev = (lon + 6) % 12, (lat + 3) % 6, (lev + 1) % 4
                    quad = (src_lon // 6) * 2 + src_lat // 3
                    at = quad * QUAD + ((src_lon % 6) * 3 + src_lat % 3) * 4 + src_lev
                    to_rolled[row, at] = 1
    return to_quads, to_rolled


def norm(values):
    center = values - jnp.mean(values, axis=-1, keepdims=True)
    spread = jnp.mean(center * center, axis=-1, keepdims=True)
    return (center * lax.rsqrt(spread + EPS)).astype(jnp.bfloat16)


def dot(a, b):
    return jnp.dot(a, b, preferred_element_type=jnp.float32)


def kernel(
    nlon, nlat,
    x_ref, qw_ref, ow_ref, uw_ref, dw_ref, tab_ref, idx_hbm, oh_hbm, quads_hbm, rolled_hbm, back_hbm,
    out_ref,
    idx_ref, quads_ref, rolled_ref, back_ref, xp, wq, wo, wu, wd, tabs, bias, nb, ho, acc, st, same, hsend, hrecv, ysend,
    own_sem, xs_sem, xr_sem, ts_sem, tr_sem, zs_sem, zr_sem, ps_sem, pr_sem, cs_sem, cr_sem,
    hs_sem, hr_sem, ys_sem, or_sem,
):
    lon, lat, head = lax.axis_index("lon"), lax.axis_index("lat"), lax.axis_index("head")

    def at(d_lon, d_lat, to_head):
        return (lax.rem(lon + d_lon + nlon, nlon), lax.rem(lat + d_lat + nlat, nlat), to_head)

    core = lax.rem(lon, 2)
    xbit = lax.rem(lon // 2, 2)
    ybit = lax.rem(lat, 2)
    x_lon = lon + 2 - 4 * xbit
    y_lat = lat + 1 - 2 * ybit
    c_lon = lon + 1 - 2 * core

    barrier = pltpu.get_barrier_semaphore()
    count = 0
    for d_lon in (-1, 0, 1):
        for d_lat in (-1, 0, 1):
            for k in range(HEADS_N):
                if d_lon == 0 and d_lat == 0 and k == 0:
                    continue
                pl.semaphore_signal(
                    barrier, inc=1, device_id=at(d_lon, d_lat, lax.rem(head + k, HEADS_N)), device_id_type=MESH
                )
                count += 1
    for target in ((x_lon, lat, head), (x_lon, y_lat, head), (lon, y_lat, head)):
        pl.semaphore_signal(barrier, inc=1, device_id=target, device_id_type=MESH)
        count += 1

    def remote(src, dst, send, recv, target):
        return pltpu.make_async_remote_copy(
            src_ref=src, dst_ref=dst, send_sem=send, recv_sem=recv, device_id=target, device_id_type=MESH
        )

    weights = ((qw_ref, wq), (ow_ref, wo), (uw_ref, wu), (dw_ref, wd))

    def part(ref, which):
        rows = ref.shape[2] // 8
        return pl.ds(pl.multiple_of(which * rows, 16), rows)

    mine = core * 4 + xbit * 2 + ybit
    of_x = core * 4 + (1 - xbit) * 2 + ybit
    of_y = core * 4 + xbit * 2 + 1 - ybit
    of_d = core * 4 + (1 - xbit) * 2 + 1 - ybit

    def x_copy(k):
        to = lax.rem(head + k, HEADS_N)
        return remote(x_ref.at[to], xp.at[head], xs_sem.at[k], xr_sem.at[k], (lon, lat, to))

    def t_copy(k):
        to = lax.rem(head + k, HEADS_N)
        return remote(tab_ref, tabs.at[head], ts_sem.at[k], tr_sem.at[k], (lon, lat, to))

    def z_copy(b, i, k):
        src, dst = weights[i]
        rows = part(dst, mine)
        to = lax.rem(head + k, HEADS_N)
        return remote(
            src.at[b, rows], dst.at[b, head, rows], zs_sem.at[b, i, k - 1], zr_sem.at[b, i, k - 1], (lon, lat, to)
        )

    def source(k):
        return lax.rem(head + HEADS_N - k, HEADS_N)

    def z_landed(b, i, k):
        dst = weights[i][1].at[b, source(k), part(weights[i][1], mine)]
        pltpu.make_async_copy(dst, dst, zr_sem.at[b, i, k - 1]).wait()

    def p_copies(b, i, k):
        ref = weights[i][1].at[b, source(k), part(weights[i][1], mine)]
        return [
            remote(ref, ref, ps_sem.at[b, i, k - 1, d], pr_sem.at[b, i, k - 1, d], target)
            for d, target in enumerate(((x_lon, lat, head), (lon, y_lat, head)))
        ]

    def p_landed(b, i, k, d):
        dst = weights[i][1].at[b, source(k), part(weights[i][1], (of_x, of_y, of_d)[d])]
        pltpu.make_async_copy(dst, dst, pr_sem.at[b, i, k - 1, d]).wait()

    def d_copy(b, i, k):
        by_x = lax.rem(b + i + k, 2)
        ref = weights[i][1].at[b, source(k), part(weights[i][1], by_x * of_x + (1 - by_x) * of_y)]
        target = (by_x * lon + (1 - by_x) * x_lon, by_x * y_lat + (1 - by_x) * lat, head)
        return remote(ref, ref, ps_sem.at[b, i, k - 1, 2], pr_sem.at[b, i, k - 1, 2], target)

    def half(ref, which):
        rows = ref.shape[2] // 2
        return pl.ds(pl.multiple_of(which * rows, 16), rows)

    def c_copy(b, i, k):
        ref = weights[i][1].at[b, source(k), half(weights[i][1], core)]
        return remote(ref, ref, cs_sem.at[b, i, k - 1], cr_sem.at[b, i, k - 1], (c_lon, lat, head))

    def c_landed(b, i, k):
        dst = weights[i][1].at[b, source(k), half(weights[i][1], 1 - core)]
        pltpu.make_async_copy(dst, dst, cr_sem.at[b, i, k - 1]).wait()

    def each_k(body):
        def step(k, carry):
            body(k)
            return carry

        lax.fori_loop(1, HEADS_N, step, 0)

    def own_copies():
        copies = [
            pltpu.make_async_copy(src, dst.at[:, head], own_sem.at[i]) for i, (src, dst) in enumerate(weights)
        ]
        copies.append(pltpu.make_async_copy(x_ref.at[head], xp.at[head], own_sem.at[4]))
        copies.append(pltpu.make_async_copy(tab_ref, tabs.at[head], own_sem.at[5]))
        small = (
            (idx_hbm, idx_ref), (quads_hbm, quads_ref), (rolled_hbm, rolled_ref), (back_hbm, back_ref),
            (oh_hbm, hsend.at[:, 512:640]),
        )
        for i, (src, dst) in enumerate(small):
            copies.append(pltpu.make_async_copy(src, dst, own_sem.at[6 + i]))
        return copies

    for copy in own_copies():
        copy.start()
    pl.semaphore_wait(barrier, count)
    each_k(lambda k: t_copy(k).start())
    each_k(lambda k: x_copy(k).start())
    order = [(b, i) for b in range(2) for i in range(4)]
    ahead = 2

    def send_along_z(t):
        if t < len(order):
            each_k(lambda k: z_copy(*order[t], k).start())

    for t in range(ahead):
        send_along_z(t)
    for copy in own_copies():
        copy.wait()

    def forward_plane(b, i):
        def body(k):
            z_landed(b, i, k)
            for copy in p_copies(b, i, k):
                copy.start()

        each_k(body)
        send_along_z(order.index((b, i)) + ahead)

    def forward_diagonal(b, i):
        def body(k):
            p_landed(b, i, k, 0)
            p_landed(b, i, k, 1)
            d_copy(b, i, k).start()

        each_k(body)

    def forward_core(b, i):
        def body(k):
            p_landed(b, i, k, 2)
            c_copy(b, i, k).start()

        each_k(body)

    def plan():
        for step in range(len(order) + 2):
            for late, forward in enumerate((forward_plane, forward_diagonal, forward_core)):
                if 0 <= step - late < len(order):
                    yield forward, order[step - late]

    pending = list(plan())

    def pump(count):
        for forward, (b, i) in pending[:count]:
            forward(b, i)
        del pending[:count]

    def make_bias(k):
        s = source(k)
        index = idx_ref[...]
        edge = jnp.concatenate([index[:, 128:], jnp.zeros((TOK, 256 - TOK), jnp.int32)], axis=1)

        def column(c, carry):
            for side, part_index in enumerate((index[:, :128], edge)):
                lo = jnp.bitwise_and(part_index, 127)
                hi = jnp.right_shift(part_index, 7)
                got = jnp.zeros((TOK, 128), jnp.float32)
                for r in range(6):
                    row = jnp.broadcast_to(tabs[s, c, r : r + 1, :], (TOK, 128))
                    got = jnp.where(hi == r, jnp.take_along_axis(row, lo, axis=1, mode="promise_in_bounds"), got)
                bias[s * 4 + c, :, side * 128 : side * 128 + 128] = got
            return carry

        lax.fori_loop(0, 4, column, 0)

    def attention(b, k):
        s = source(k)
        n = nb[...]
        query = (dot(n, wq[b, s, 0:512, :]) * 0.125).astype(jnp.bfloat16)
        keys = dot(n, wq[b, s, 512:1024, :]).astype(jnp.bfloat16)
        v = dot(n, wq[b, s, 1024:1536, :]).astype(jnp.bfloat16)
        for w in range(2):
            rows = slice(w * TOK, (w + 1) * TOK)
            outs = []
            for hh in range(2):
                cols = slice(hh * 64, hh * 64 + 64)
                scores = lax.dot_general(
                    query[rows, cols], keys[rows, cols], (((1,), (1,)), ((), ())),
                    preferred_element_type=jnp.float32,
                )
                scores = scores + bias[s * 4 + b * 2 + hh, :, 0:TOK]
                if b == 1:
                    scores = jnp.where(same[w] > 0.5, scores, MASKED)
                expo = jnp.exp(scores - jnp.max(scores, axis=-1, keepdims=True))
                probs = (expo * (1.0 / jnp.sum(expo, axis=-1, keepdims=True))).astype(jnp.bfloat16)
                outs.append(dot(probs, v[rows, cols]).astype(jnp.bfloat16))
            ho[rows, :] = jnp.concatenate(outs, axis=1)
        total = dot(ho[...], wo[b, s])
        acc[...] = total if k == 0 else acc[...] + total

    def feed_forward(b, k):
        s = source(k)
        hidden = jax.nn.gelu(dot(nb[...], wu[b, s]), approximate=True).astype(jnp.bfloat16)
        total = dot(hidden, wd[b, s])
        acc[...] = total if k == 0 else acc[...] + total

    def add_total():
        st[...] = (st[...].astype(jnp.float32) + acc[...]).astype(jnp.bfloat16)

    def renorm():
        nb[...] = norm(st[...].astype(jnp.float32))

    pump(1)
    each_k(lambda k: pltpu.make_async_copy(xp.at[source(k)], xp.at[source(k)], xr_sem.at[k]).wait())
    st[...] = jnp.concatenate([xp[g] for g in range(4)], axis=1)
    renorm()
    pump(2)
    make_bias(0)
    pump(3)
    attention(0, 0)
    pump(1)
    each_k(lambda k: pltpu.make_async_copy(tabs.at[source(k)], tabs.at[source(k)], tr_sem.at[k]).wait())
    make_bias(1)
    pump(1)
    make_bias(2)
    pump(1)
    make_bias(3)
    for k in range(1, 4):
        c_landed(0, 0, k)
        c_landed(0, 1, k)
        attention(0, k)
        pump(2)
    add_total()
    renorm()
    for k in range(4):
        if k > 0:
            c_landed(0, 2, k)
            c_landed(0, 3, k)
        feed_forward(0, k)
        pump(1)
    add_total()

    hsend[:, 0:512] = dot(quads_ref[...], st[...]).astype(jnp.bfloat16)
    before = lax.rem(head + HEADS_N - 1, HEADS_N)
    lat_back = jnp.where(head == 0, -1, 0)
    lat_next = jnp.where(head == HEADS_N - 1, 1, 0)
    quad_to = (at(-1, lat_back, before), at(-1, 0, head), at(0, lat_back, before))

    def quad_rows(q):
        return pl.ds(q * QUAD, QUAD)

    halo = [
        remote(hsend.at[quad_rows(q)], hrecv.at[quad_rows(q)], hs_sem.at[q], hr_sem.at[q], quad_to[q])
        for q in range(3)
    ]
    for copy in halo:
        copy.start()
    hrecv[3 * QUAD : 4 * QUAD, :] = hsend[3 * QUAD : 4 * QUAD, :]
    pump(2)
    for copy in halo:
        copy.wait()

    rolled = dot(rolled_ref[...], hrecv[...]).astype(jnp.bfloat16)
    st[...] = rolled[:, 0:512]
    marks = rolled[:, 512:640]
    for w in range(2):
        of_window = marks[w * TOK : (w + 1) * TOK]
        same[w] = lax.dot_general(
            of_window, of_window, (((1,), (1,)), ((), ())), preferred_element_type=jnp.float32
        )
    renorm()
    attention(1, 0)
    pump(1)
    for k in range(1, 4):
        c_landed(1, 0, k)
        c_landed(1, 1, k)
        attention(1, k)
        pump(1)
    add_total()
    renorm()
    for k in range(4):
        if k > 0:
            c_landed(1, 2, k)
            c_landed(1, 3, k)
        feed_forward(1, k)
    add_total()

    final = dot(back_ref[...], st[...]).astype(jnp.bfloat16)
    for f in range(4):
        ysend[f] = final[:, f * 128 : (f + 1) * 128]
    after = lax.rem(head + 1, HEADS_N)
    homes = ((1, lat_next, after), (1, 0, head), (0, lat_next, after), (0, 0, head))

    def y_copy(q, k):
        d_lon, d_lat, slot = homes[q]
        to = lax.rem(head + k, HEADS_N)
        return remote(
            ysend.at[to, quad_rows(q)], out_ref.at[slot, quad_rows(q)], ys_sem.at[q, k], or_sem.at[slot, q],
            at(d_lon, d_lat, to),
        )

    def y_local(q):
        slot = homes[q][2]
        return pltpu.make_async_copy(
            ysend.at[head, quad_rows(q)], out_ref.at[slot, quad_rows(q)], or_sem.at[slot, q]
        )

    for q in range(4):
        each_k(lambda k: y_copy(q, k).start())
    for q in (0, 1):
        y_copy(q, 0).start()
    y_local(3).start()

    @pl.when(head < HEADS_N - 1)
    def _():
        y_local(2).start()

    @pl.when(head == HEADS_N - 1)
    def _():
        y_copy(2, 0).start()

    each_k(lambda k: t_copy(k).wait_send())
    each_k(lambda k: x_copy(k).wait_send())
    for b in range(2):
        for i in range(4):

            def sent(k):
                z_copy(b, i, k).wait_send()
                for copy in p_copies(b, i, k):
                    copy.wait_send()
                d_copy(b, i, k).wait_send()
                c_copy(b, i, k).wait_send()

            each_k(sent)
    for q in range(4):
        each_k(lambda k: y_copy(q, k).wait_send())
    for q in (0, 1):
        y_copy(q, 0).wait_send()

    @pl.when(head == HEADS_N - 1)
    def _():
        y_copy(2, 0).wait_send()

    for g in range(4):
        for q in range(4):
            dst = out_ref.at[g, quad_rows(q)]
            pltpu.make_async_copy(dst, dst, or_sem.at[g, q]).wait()


def local(
    nlon, nlat, tokens, qkv_weight, out_weight, up_weight, down_weight, bias_table, bias_index, regions
):
    bf16 = jnp.bfloat16
    head = lax.axis_index("head")
    to_quads, to_rolled = row_maps()
    x = tokens.reshape(12, 4, 6, 2, 2, 128).transpose(1, 3, 0, 2, 4, 5).reshape(4, ROWS, 128)
    table = jnp.pad(bias_table, ((0, 0), (0, 1024 - bias_table.shape[1]), (0, 0)))
    table = table.transpose(0, 2, 1).reshape(4, 8, 128)
    ids = lax.dynamic_slice_in_dim(regions, head * 6, 6, axis=1)
    ids = ids.reshape(2, 6, 2, 3, 4).transpose(0, 2, 1, 3, 4).reshape(4, 72)
    ids = jnp.pad(ids, ((0, 0), (0, QUAD - 72))).reshape(4 * QUAD, 1)
    marks = (ids == jnp.arange(128, dtype=jnp.int32)[None, :]).astype(bf16)
    sems = pltpu.SemaphoreType.DMA
    vm = pltpu.VMEM
    any_space = pl.BlockSpec(memory_space=pl.ANY)
    in_hbm = pl.BlockSpec(memory_space=pltpu.HBM)
    out = pl.pallas_call(
        functools.partial(kernel, nlon, nlat),
        out_shape=jax.ShapeDtypeStruct((4, 4 * QUAD, 128), bf16),
        in_specs=[any_space] + [in_hbm] * 4 + [any_space] + [in_hbm] + [any_space] + [in_hbm] * 3,
        out_specs=any_space,
        scratch_shapes=[
            vm((TOK, TOK), jnp.int32),
            vm((4 * QUAD, ROWS), bf16),
            vm((ROWS, 4 * QUAD), bf16),
            vm((4 * QUAD, ROWS), bf16),
            vm((4, ROWS, 128), bf16),
            vm((2, 4, 1536, 128), bf16),
            vm((2, 4, 128, 512), bf16),
            vm((2, 4, 512, 512), bf16),
            vm((2, 4, 512, 512), bf16),
            vm((4, 4, 8, 128), jnp.float32),
            vm((16, TOK, 256), jnp.float32),
            vm((ROWS, 512), bf16),
            vm((ROWS, 128), bf16),
            vm((ROWS, 512), jnp.float32),
            vm((ROWS, 512), bf16),
            vm((2, TOK, TOK), jnp.float32),
            vm((4 * QUAD, 640), bf16),
            vm((4 * QUAD, 640), bf16),
            vm((4, 4 * QUAD, 128), bf16),
            sems((11,)),
            sems((4,)),
            sems((4,)),
            sems((4,)),
            sems((4,)),
            sems((2, 4, 3)),
            sems((2, 4, 3)),
            sems((2, 4, 3, 3)),
            sems((2, 4, 3, 3)),
            sems((2, 4, 3)),
            sems((2, 4, 3)),
            sems((3,)),
            sems((3,)),
            sems((4, 4)),
            sems((4, 4)),
        ],
        compiler_params=pltpu.CompilerParams(
            collective_id=0, has_side_effects=True, vmem_limit_bytes=48 * 1024 * 1024
        ),
        name="swin_pair",
    )(
        x,
        qkv_weight.reshape(2, 1536, 128),
        out_weight,
        up_weight,
        down_weight,
        table,
        bias_index,
        marks,
        jnp.asarray(to_quads, bf16),
        jnp.asarray(to_rolled, bf16),
        jnp.asarray(to_rolled.T, bf16),
    )
    out = out.reshape(4, 4, QUAD, 128)[:, :, :72].reshape(4, 2, 2, 6, 3, 4, 128)
    return out.transpose(1, 3, 0, 2, 4, 5, 6).reshape(12, 24, 4, 128)


def solution(mesh):
    return jax.shard_map(
        functools.partial(local, mesh.shape["lon"], mesh.shape["lat"]),
        mesh=mesh,
        in_specs=(
            P("lon", "lat", None, "head"),
            P(None, None, None, "head"),
            P(None, "head", None),
            P(None, None, "head"),
            P(None, "head", None),
            P(None, None, "head"),
            P(),
            P("lon", "lat", None),
        ),
        out_specs=P("lon", "lat", None, "head"),
        check_vma=False,
    )
```
